256 devices in a mesh: cuts: 2 (over x_hi), fsdp: 32 (over z, y), tp: 4 (over x_lo, core).
Axes of the slice: x: 4 (x_hi: 2, x_lo: 2; x = x_hi * 2 + x_lo), y: 4, z: 8, core: 2. Of those that a mesh axis runs over, the one named last changes fastest.
Arguments:
- hidden: bfloat16 [10240, 14336], P(('cuts', 'fsdp'), 'tp'), may hold values from -6 to 6
- grad_out: bfloat16 [10240, 4096], P(('cuts', 'fsdp'), 'tp'), may hold values from -16 to 16
- weight: bfloat16 [2, 4096, 14336], P('cuts', 'fsdp', 'tp'), may hold values from -6 to 6
- anchor: float32 [4096, 14336], P('fsdp', 'tp'), may hold values from -6 to 6
- momentum: float32 [4096, 14336], P('fsdp', 'tp'), may hold values from -3 to 3
Outputs:
- grad_hidden: bfloat16 [10240, 14336], P(('cuts', 'fsdp'), 'tp')
- mixed: bfloat16 [2, 4096, 14336], P('cuts', 'fsdp', 'tp')
- new_anchor: float32 [4096, 14336], P('fsdp', 'tp')
- new_momentum: float32 [4096, 14336], P('fsdp', 'tp')
The draws below stay inside these ranges and needn't reach their ends.
All inputs are finite; a program needn't handle non-finite values.
Results may differ from the reference program's by a relative error of at most 0.024.
Values may be sent and summed in bfloat16 or wider, within the bound.
No kernel may reach another device: no remote copies, remote signals or barrier semaphores. Data moves between devices by JAX's collectives and lax.ppermute only.
A program may use at most 192 MiB of HBM per device.

```python
import jax
import jax.numpy as jnp
from jax import lax

D = 4096
FF = 14336
TOK_DEV = 160
REPLICAS = 2
TOKENS = 10240
N_CUTS = 2
N_FSDP = 32


def strengthened(result, own_key, source, target, blocks, factor):
    owner, partner = [(jnp.arange(result.shape[axis_at]) // (result.shape[axis_at] // blocks)).reshape([-1 if axis == axis_at else 1 for axis in range(result.ndim)]) for axis_at in (source, target)]
    chosen = jax.random.permutation(own_key, blocks)[partner]
    strong = (owner == chosen) | (owner == (partner + blocks // 2) % blocks)
    return jnp.where(strong, factor * result, result)


def steps_of(stream_key, dims, split, least, largest):
    loudness, own = 1.0, jax.random.fold_in(stream_key, 6)
    for position, shards_of in split:
        steps = jnp.exp(jax.random.uniform(jax.random.fold_in(own, position), (shards_of,), jnp.float32, least / len(split), largest / len(split)))
        loudness = loudness * jnp.repeat(steps, dims[position] // shards_of).reshape([-1 if axis == position else 1 for axis in range(len(dims))])
    return loudness


def centred(own_key, extent, width, limit, split=(), dtype=jnp.bfloat16):
    array = width * jax.random.normal(own_key, extent, jnp.float32)
    if split:
        array = array * steps_of(own_key, extent, split, -0.22, 0.18)
    return jnp.clip(array, -limit, limit).astype(dtype)


def gaussian_with(stream_key, extent, deviation, reach, shards, heavy, dtype=jnp.bfloat16):
    entries = deviation * jax.random.normal(stream_key, extent, jnp.float32)
    if shards:
        entries = entries * steps_of(stream_key, extent, shards, -0.22, 0.18)
    return jnp.clip(strengthened(entries, jax.random.fold_in(stream_key, 3), *heavy), -reach, reach).astype(dtype)


def setup_inputs(seed: int = 0) -> dict:
    key_list = jax.random.split(jax.random.key(seed), 6)
    hidden = centred(key_list[0], (TOKENS, FF), 1.0, 6.0, ((0, 64), (1, 4)))
    grad_out = gaussian_with(key_list[1], (TOKENS, D), 1.0, 16.0, ((0, 64), (1, 4)), (0, 1, 64, 4.0))
    weight = centred(key_list[2], (REPLICAS, D, FF), 1.0, 6.0, ((0, 2), (1, 32), (2, 4)))
    anchor = centred(key_list[3], (D, FF), 1.0, 6.0, ((0, 32), (1, 4)), jnp.float32)
    momentum = centred(key_list[4], (D, FF), 0.5, 3.0, ((0, 32), (1, 4)), jnp.float32)
    return {"hidden": hidden, "grad_out": grad_out, "weight": weight, "anchor": anchor, "momentum": momentum}


inner_rate = 1.0
outer_rate = 0.7
momentum_decay = 0.9
mix_weight = 0.5


def reference(hidden, grad_out, weight, anchor, momentum):
    factor = FF ** -0.5
    rows = TOK_DEV * N_FSDP
    dh_list = []
    inner_list = []
    total = jnp.zeros((D, FF), jnp.float32)
    for replica in range(N_CUTS):
        h_rep = hidden[replica * rows:(replica + 1) * rows].astype(jnp.float32)
        g_rep = grad_out[replica * rows:(replica + 1) * rows].astype(jnp.float32)
        w_rep = weight[replica].astype(jnp.float32)
        dh_list.append((factor * jnp.dot(g_rep, w_rep, precision=lax.Precision.HIGHEST)).astype(jnp.bfloat16))
        h_blocks = h_rep.reshape(N_FSDP, TOK_DEV, FF)
        g_blocks = g_rep.reshape(N_FSDP, TOK_DEV, D)

        def add_block(carry, pair):
            g_block, h_block = pair
            term = (factor * jnp.dot(g_block.T, h_block, precision=lax.Precision.HIGHEST)).astype(jnp.bfloat16)
            term = lax.optimization_barrier(term)
            return carry + term.astype(jnp.float32), None

        grad_w, unused = lax.scan(add_block, jnp.zeros((D, FF), jnp.float32), (g_blocks, h_blocks))
        inner = (w_rep - inner_rate * grad_w).astype(jnp.bfloat16)
        inner_list.append(inner)
        delta = (anchor - inner.astype(jnp.float32)).astype(jnp.bfloat16)
        delta = lax.optimization_barrier(delta)
        total = total + delta.astype(jnp.float32)
    average = total / N_CUTS
    new_momentum = momentum_decay * momentum + average
    new_anchor = anchor - outer_rate * (average + momentum_decay * new_momentum)
    mixed = jnp.stack([(mix_weight * inner.astype(jnp.float32) + (1.0 - mix_weight) * new_anchor).astype(jnp.bfloat16) for inner in inner_list])
    grad_hidden = jnp.concatenate(dh_list, axis=0)
    return grad_hidden, mixed, new_anchor, new_momentum
```

```python
import jax
import jax.numpy as jnp
from jax import lax
from jax.sharding import Mesh
from jax.sharding import PartitionSpec as P

inner_rate = 1.0
outer_rate = 0.7
momentum_decay = 0.9
mix_weight = 0.5

Z, Y = 8, 4
f32, bf16 = jnp.float32, jnp.bfloat16


def shift(x, axis, by):
    n = lax.axis_size(axis)
    return lax.ppermute(x, axis, [(i, (i + by) % n) for i in range(n)])


def cross(x, by):
    perm = [(c * Y + i, (1 - c) * Y + (i + by) % Y) for c in range(2) for i in range(Y)]
    return lax.ppermute(x, ("cuts", "y"), perm)


def local(hidden, grad_out, weight, anchor, momentum):
    width = hidden.shape[1]
    factor = (width * 4) ** (-0.5)
    z, y = lax.axis_index("z"), lax.axis_index("y")
    t = lax.axis_index("xl") * 2 + lax.axis_index("core")
    part = width // Y
    rows = weight.shape[1]
    deep = rows * Y
    toks = hidden.shape[0]
    local_w = weight[0]

    def columns(x, k):
        return lax.dynamic_slice_in_dim(x, k % Y * part, part, axis=1)

    def band(x, k):
        return lax.dynamic_slice_in_dim(x, k % Y * rows, rows, axis=0)

    w_parts = [columns(local_w, y)] + [shift(columns(local_w, y + d), "y", d) for d in (1, 2, 3)]
    g_rows = jnp.concatenate([grad_out] + [shift(grad_out, "y", d) for d in (1, 2, 3)], axis=0)
    h_mine = jnp.concatenate(
        [columns(hidden, y)] + [shift(columns(hidden, y + d), "y", d) for d in (1, 2, 3)], axis=0
    )
    w_mine = jnp.zeros((deep, part), bf16)
    for d in range(Y):
        w_mine = lax.dynamic_update_slice_in_dim(w_mine, w_parts[d], (y - d) % Y * rows, axis=0)

    g_far = shift(g_rows, "xl", 1)
    g_all = jnp.stack([g_rows, shift(g_rows, "core", 1), g_far, shift(g_far, "core", 1)])

    def features(k):
        k = k % Z
        per = grad_out.shape[1] // deep
        return lax.dynamic_slice(g_all, ((k // per) ^ t, 0, k % per * deep), (1, Y * toks, deep))[0]

    def term(k):
        return factor * lax.dot_general(
            features(k), h_mine, (((0,), (0,)), ((), ())), preferred_element_type=f32
        )

    half = deep // 2
    far = term(z + 4).astype(bf16)
    up, down = shift(far[:half], "z", 1), shift(far[half:], "z", -1)
    b = term(z + 3)
    up = jnp.concatenate([b[:half] + up.astype(f32), b[half:]], axis=0)
    b = term(z - 3)
    down = jnp.concatenate([b[:half], b[half:] + down.astype(f32)], axis=0)
    up, down = shift(up.astype(bf16), "z", 1), shift(down.astype(bf16), "z", -1)
    for k in (2, 1):
        up = (term(z + k) + up.astype(f32)).astype(bf16)
        down = (term(z - k) + down.astype(f32)).astype(bf16)
        up, down = shift(up, "z", 1), shift(down, "z", -1)
    grad_w = term(z) + up.astype(f32) + down.astype(f32)
    inner_t = (w_mine.astype(f32) - inner_rate * grad_w).astype(bf16)

    def product(k, w_block):
        return jnp.dot(features(k), w_block, preferred_element_type=f32)

    total = product(z, w_mine)
    up, down = w_mine, w_mine
    for k in (1, 2, 3):
        up, down = shift(up, "z", 1), shift(down, "z", -1)
        total = total + product(z - k, up) + product(z + k, down)
    up, down = shift(up[:half], "z", 1), shift(down[half:], "z", -1)
    total = total + product(z + 4, jnp.concatenate([up, down], axis=0))
    grad_h = (factor * total).astype(bf16)
    grad_hidden = jnp.zeros(hidden.shape, bf16)
    for d in range(Y):
        piece = grad_h[d * toks : (d + 1) * toks]
        if d:
            piece = shift(piece, "y", -d)
        grad_hidden = lax.dynamic_update_slice_in_dim(grad_hidden, piece, (y + d) % Y * part, axis=1)

    inner = jnp.zeros(local_w.shape, bf16)
    other = jnp.zeros(local_w.shape, bf16)
    for d in range(Y):
        piece = band(inner_t, y + d)
        mine = shift(piece, "y", d) if d else piece
        inner = lax.dynamic_update_slice_in_dim(inner, mine, (y - d) % Y * part, axis=1)
        other = lax.dynamic_update_slice_in_dim(other, cross(piece, d), (y - d) % Y * part, axis=1)

    def delta(x):
        return (anchor - x.astype(f32)).astype(bf16).astype(f32)

    average = (delta(inner) + delta(other)) / lax.axis_size("cuts")
    new_momentum = momentum_decay * momentum + average
    new_anchor = anchor - outer_rate * (average + momentum_decay * new_momentum)
    mixed = (mix_weight * inner.astype(f32) + (1.0 - mix_weight) * new_anchor).astype(bf16)
    return (grad_hidden, mixed[None], new_anchor, new_momentum)


def solution(mesh):
    grid = Mesh(mesh.devices.reshape(2, Z, Y, 2, 2), ("cuts", "z", "y", "xl", "core"))
    tokens, rows, units = P(("cuts", "z", "y"), ("xl", "core")), ("z", "y"), ("xl", "core")
    return jax.shard_map(
        local,
        mesh=grid,
        in_specs=(tokens, tokens, P("cuts", rows, units), P(rows, units), P(rows, units)),
        out_specs=(tokens, P("cuts", rows, units), P(rows, units), P(rows, units)),
        check_vma=False,
    )
```

```python
import jax
import jax.numpy as jnp
from jax import lax
from jax.sharding import Mesh
from jax.sharding import PartitionSpec as P

inner_rate = 1.0
outer_rate = 0.7
momentum_decay = 0.9
mix_weight = 0.5

Z, Y = 8, 4
f32, bf16 = jnp.float32, jnp.bfloat16
tie = lax.optimization_barrier


def shift(x, axis, by):
    n = lax.axis_size(axis)
    return lax.ppermute(x, axis, [(i, (i + by) % n) for i in range(n)])


def cross(x, by):
    perm = [(c * Y + i, (1 - c) * Y + (i + by) % Y) for c in range(2) for i in range(Y)]
    return lax.ppermute(x, ("cuts", "y"), perm)


def local(hidden, grad_out, weight, anchor, momentum):
    width = hidden.shape[1]
    factor = (width * 4) ** (-0.5)
    z, y = lax.axis_index("z"), lax.axis_index("y")
    t = lax.axis_index("xl") * 2 + lax.axis_index("core")
    part = width // Y
    rows = weight.shape[1]
    deep = rows * Y
    toks = hidden.shape[0]
    local_w = weight[0]
    half = deep // 2

    def columns(x, k):
        return lax.dynamic_slice_in_dim(x, k % Y * part, part, axis=1)

    def band(x, k):
        return lax.dynamic_slice_in_dim(x, k % Y * rows, rows, axis=0)

    g_all = lax.all_gather(grad_out, ("y", "xl", "core")).reshape(Y, -1, toks, grad_out.shape[1])
    per = grad_out.shape[1] // deep

    def features(k):
        k = k % Z
        at, size = (0, k // per, 0, k % per * deep), (Y, 1, toks, deep)
        return lax.dynamic_slice(g_all, at, size).reshape(Y * toks, deep)

    def gathered(x):
        parts = {d: shift(columns(x, y + d), "y", d) for d in (2, 1, 3)}
        parts[0] = columns(x, y)
        n = x.shape[0]
        whole = jnp.zeros((Y * n, part), bf16)
        for d in (0, 1, 3, 2):
            whole = lax.dynamic_update_slice_in_dim(whole, parts[d], (y - d) % Y * n, axis=0)
        return whole

    w_mine = gathered(local_w)
    h_sent = jnp.stack([hidden[:, k * part : (k + 1) * part] for k in range(Y)])
    h_mine = lax.all_to_all(h_sent, "y", 0, 0, tiled=True).reshape(Y * toks, part)

    ups, downs = [w_mine], [w_mine]
    for k in (1, 2):
        ups.append(shift(ups[-1], "z", 1))
        downs.append(shift(downs[-1], "z", -1))
    ups[2], downs[2], h_mine = tie((ups[2], downs[2], h_mine))
    ups.append(shift(ups[2], "z", 1))
    downs.append(shift(downs[2], "z", -1))

    def term(k):
        return factor * lax.dot_general(
            features(k), h_mine, (((0,), (0,)), ((), ())), preferred_element_type=f32
        )

    def product(k, w_block):
        return jnp.dot(features(k), w_block, preferred_element_type=f32)

    far = term(z + 4).astype(bf16)
    up, down = shift(far[:half], "z", 1), shift(far[half:], "z", -1)
    up, down, ups[3], downs[3] = tie((up, down, ups[3], downs[3]))
    b = term(z + 3)
    up = jnp.concatenate([b[:half] + up.astype(f32), b[half:]], axis=0)
    b = term(z - 3)
    down = jnp.concatenate([b[:half], b[half:] + down.astype(f32)], axis=0)
    up, down = shift(up.astype(bf16), "z", 1), shift(down.astype(bf16), "z", -1)
    last = [shift(ups[3][:half], "z", 1), shift(downs[3][half:], "z", -1)]
    total = product(z, w_mine)
    for k in (1, 2, 3):
        total = total + product(z - k, ups[k]) + product(z + k, downs[k])
    up, down, total, last = tie((up, down, total, last))
    up = (term(z + 2) + up.astype(f32)).astype(bf16)
    down = (term(z - 2) + down.astype(f32)).astype(bf16)
    up, down = shift(up, "z", 1), shift(down, "z", -1)

    total = total + product(z + 4, jnp.concatenate(last, axis=0))
    grad_h = (factor * total).astype(bf16)
    back = lax.all_to_all(grad_h.reshape(Y, toks, part), "y", 0, 0, tiled=True)
    up, down, back = tie((up, down, back))
    grad_hidden = jnp.concatenate([back[k] for k in range(Y)], axis=1)

    up = (term(z + 1) + up.astype(f32)).astype(bf16)
    down = (term(z - 1) + down.astype(f32)).astype(bf16)
    up, down = shift(up, "z", 1), shift(down, "z", -1)
    grad_w = term(z) + up.astype(f32) + down.astype(f32)
    inner_t = (w_mine.astype(f32) - inner_rate * grad_w).astype(bf16)

    sent = jnp.concatenate([inner_t, inner_t], axis=0).reshape(2 * Y, rows, part)
    got = lax.all_to_all(sent, ("cuts", "y"), 0, 0, tiled=True)
    c = lax.axis_index("cuts")

    def of(c):
        blocks = lax.dynamic_slice_in_dim(got, c * Y, Y, axis=0)
        return jnp.concatenate([blocks[k] for k in range(Y)], axis=1)

    inner, other = of(c), of(1 - c)

    def delta(x):
        return (anchor - x.astype(f32)).astype(bf16).astype(f32)

    average = (delta(inner) + delta(other)) / lax.axis_size("cuts")
    new_momentum = momentum_decay * momentum + average
    new_anchor = anchor - outer_rate * (average + momentum_decay * new_momentum)
    mixed = (mix_weight * inner.astype(f32) + (1.0 - mix_weight) * new_anchor).astype(bf16)

    return (grad_hidden, mixed[None], new_anchor, new_momentum)


def solution(mesh):
    grid = Mesh(mesh.devices.reshape(2, Z, Y, 2, 2), ("cuts", "z", "y", "xl", "core"))
    tokens, rows, units = P(("cuts", "z", "y"), ("xl", "core")), ("z", "y"), ("xl", "core")
    return jax.shard_map(
        local,
        mesh=grid,
        in_specs=(tokens, tokens, P("cuts", rows, units), P(rows, units), P(rows, units)),
        out_specs=(tokens, P("cuts", rows, units), P(rows, units), P(rows, units)),
        check_vma=False,
    )
```

```python
import jax
import jax.numpy as jnp
from jax import lax
from jax.sharding import Mesh
from jax.sharding import PartitionSpec as P

inner_rate = 1.0
outer_rate = 0.7
momentum_decay = 0.9
mix_weight = 0.5

Z, Y = 8, 4
f32, bf16 = jnp.float32, jnp.bfloat16
tie = lax.optimization_barrier


def shift(x, axis, by):
    n = lax.axis_size(axis)
    return lax.ppermute(x, axis, [(i, (i + by) % n) for i in range(n)])


def cross(x, by):
    perm = [(c * Y + i, (1 - c) * Y + (i + by) % Y) for c in range(2) for i in range(Y)]
    return lax.ppermute(x, ("cuts", "y"), perm)


def local(hidden, grad_out, weight, anchor, momentum):
    width = hidden.shape[1]
    factor = (width * 4) ** (-0.5)
    z, y = lax.axis_index("z"), lax.axis_index("y")
    t = lax.axis_index("xl") * 2 + lax.axis_index("core")
    part = width // Y
    rows = weight.shape[1]
    deep = rows * Y
    toks = hidden.shape[0]
    local_w = weight[0]
    half = deep // 2

    def columns(x, k):
        return lax.dynamic_slice_in_dim(x, k % Y * part, part, axis=1)

    def band(x, k):
        return lax.dynamic_slice_in_dim(x, k % Y * rows, rows, axis=0)

    g_all = lax.all_gather(grad_out, ("y", "xl", "core")).reshape(Y, -1, toks, grad_out.shape[1])
    per = grad_out.shape[1] // deep

    def features(k):
        k = k % Z
        at, size = (0, k // per, 0, k % per * deep), (Y, 1, toks, deep)
        return lax.dynamic_slice(g_all, at, size).reshape(Y * toks, deep)

    def gathered(x):
        parts = {d: shift(columns(x, y + d), "y", d) for d in (2, 1, 3)}
        parts[0] = columns(x, y)
        n = x.shape[0]
        whole = jnp.zeros((Y * n, part), bf16)
        for d in (0, 1, 3, 2):
            whole = lax.dynamic_update_slice_in_dim(whole, parts[d], (y - d) % Y * n, axis=0)
        return whole

    w_mine = gathered(local_w)
    h_sent = jnp.stack([hidden[:, k * part : (k + 1) * part] for k in range(Y)])
    h_mine = lax.all_to_all(h_sent, "y", 0, 0, tiled=True).reshape(Y * toks, part)

    spans = ((0, 512), (512, part))
    ups = [[w_mine[:, a:b] for a, b in spans]]
    downs = [ups[0]]
    for k in (1, 2):
        ups.append([shift(x, "z", 1) for x in ups[-1]])
        downs.append([shift(x, "z", -1) for x in downs[-1]])
    ups[2], downs[2], h_mine = tie((ups[2], downs[2], h_mine))
    ups.append([shift(x, "z", 1) for x in ups[2]])
    downs.append([shift(x, "z", -1) for x in downs[2]])

    def term(k):
        return factor * lax.dot_general(
            features(k), h_mine, (((0,), (0,)), ((), ())), preferred_element_type=f32
        )

    def product(k, w_block):
        return jnp.dot(features(k), w_block, preferred_element_type=f32)

    far = term(z + 4).astype(bf16)
    up, down = shift(far[:half], "z", 1), shift(far[half:], "z", -1)
    up, down, ups[3], downs[3] = tie((up, down, ups[3], downs[3]))
    b = term(z + 3)
    up = jnp.concatenate([b[:half] + up.astype(f32), b[half:]], axis=0)
    b = term(z - 3)
    down = jnp.concatenate([b[:half], b[half:] + down.astype(f32)], axis=0)
    up, down = shift(up.astype(bf16), "z", 1), shift(down.astype(bf16), "z", -1)
    last = [
        shift(jnp.concatenate([x[:half] for x in ups[3]], axis=1), "z", 1),
        shift(jnp.concatenate([x[half:] for x in downs[3]], axis=1), "z", -1),
    ]
    total = []
    for p in range(2):
        summed = product(z, ups[0][p])
        for k in (1, 2, 3):
            summed = summed + product(z - k, ups[k][p]) + product(z + k, downs[k][p])
        total.append(summed)
    up, down, total, last = tie((up, down, total, last))
    up = (term(z + 2) + up.astype(f32)).astype(bf16)
    down = (term(z - 2) + down.astype(f32)).astype(bf16)
    up, down = shift(up, "z", 1), shift(down, "z", -1)

    total = jnp.concatenate(total, axis=1) + product(z + 4, jnp.concatenate(last, axis=0))
    grad_h = (factor * total).astype(bf16)
    back = lax.all_to_all(grad_h.reshape(Y, toks, part), "y", 0, 0, tiled=True)
    up, down, back = tie((up, down, back))
    grad_hidden = jnp.concatenate([back[k] for k in range(Y)], axis=1)

    up = (term(z + 1) + up.astype(f32)).astype(bf16)
    down = (term(z - 1) + down.astype(f32)).astype(bf16)
    up, down = shift(up, "z", 1), shift(down, "z", -1)
    grad_w = term(z) + up.astype(f32) + down.astype(f32)
    inner_t = (w_mine.astype(f32) - inner_rate * grad_w).astype(bf16)

    sent = jnp.concatenate([inner_t, inner_t], axis=0).reshape(2 * Y, rows, part)
    got = lax.all_to_all(sent, ("cuts", "y"), 0, 0, tiled=True)
    c = lax.axis_index("cuts")

    def of(c):
        blocks = lax.dynamic_slice_in_dim(got, c * Y, Y, axis=0)
        return jnp.concatenate([blocks[k] for k in range(Y)], axis=1)

    inner, other = of(c), of(1 - c)

    def delta(x):
        return (anchor - x.astype(f32)).astype(bf16).astype(f32)

    average = (delta(inner) + delta(other)) / lax.axis_size("cuts")
    new_momentum = momentum_decay * momentum + average
    new_anchor = anchor - outer_rate * (average + momentum_decay * new_momentum)
    mixed = (mix_weight * inner.astype(f32) + (1.0 - mix_weight) * new_anchor).astype(bf16)

    return (grad_hidden, mixed[None], new_anchor, new_momentum)


def solution(mesh):
    grid = Mesh(mesh.devices.reshape(2, Z, Y, 2, 2), ("cuts", "z", "y", "xl", "core"))
    tokens, rows, units = P(("cuts", "z", "y"), ("xl", "core")), ("z", "y"), ("xl", "core")
    return jax.shard_map(
        local,
        mesh=grid,
        in_specs=(tokens, tokens, P("cuts", rows, units), P(rows, units), P(rows, units)),
        out_specs=(tokens, P("cuts", rows, units), P(rows, units), P(rows, units)),
        check_vma=False,
    )
```
